32 devices in a mesh: groups: 2 (over y), ctx: 4 (over z), dp: 2 (over x), mp: 2 (over core).
Axes of the slice: x: 2, y: 2, z: 4, core: 2. Of those that a mesh axis runs over, the one named last changes fastest.
Arguments:
- teacher_rows: bfloat16 [2, 8192, 4096], P('dp', ('groups', 'ctx'), 'mp'), parts along dimension 1, may hold values from -6 to 6
- student_hidden: bfloat16 [2, 6144, 1536], P('dp', ('groups', 'ctx'), 'mp'), parts along dimension 1, may hold values from -6 to 6
- projector: bfloat16 [4096, 1536], P(None, 'mp'), may hold values from -0.09375 to 0.09375
- span_end: int32 [2, 6144], P('dp', ('groups', 'ctx')), parts along dimension 1, may hold values from 1 to 4096, as said below
Outputs:
- token_loss: float32 [2, 6144], P('dp', ('groups', 'ctx')), parts along dimension 1
- w_grad: float32 [8192, 1536], P(('groups', 'ctx', 'dp'), 'mp'), parts along dimension 0
The draws below stay inside these ranges and needn't reach their ends.
There are 2 independent parts, one for each index of `groups`. The reference program is written for one: setup_inputs(seed, part) draws one part's arguments, and reference() takes and returns one part's arrays. A program takes and returns all parts, laid end to end along the dimension named above; an argument that names none is the same for every part. Nothing has to cross between parts.
Inputs may be any that keep to these rules, and one draw needn't show every extreme that they name: `span_end`: ends rise by 1 or more from token to token and the last of a document is 4096. The end of student token i * 768 - 1 lies within 128 of i * 1024 for every i, and in every document it is exactly i * 1024 + 128 or i * 1024 - 128 for some i. Student token i * 768 spans exactly one teacher token for every i.
All inputs are finite; a program needn't handle non-finite values.
Results may differ from the reference program's by a relative error of at most 0.0033.
Values may be sent and summed in bfloat16 or wider, within the bound.
A program may use at most 128 MiB of HBM per device.

```python
import jax
import jax.numpy as jnp
from jax import lax

D = 4096
E = 1536
TT = 1024
SS = 768
HW = 128
DOCS = 2
TLEN = 4096
SLEN = 3072
N_CTX = 4


def draw_span_end(key, part):
    key = jax.random.fold_in(key, 11)
    key_shift, key_pick, key_sign, key_slots = jax.random.split(key, 4)
    shifts = jax.random.randint(key_shift, (DOCS, N_CTX - 1), -HW, HW + 1).astype(jnp.int32)
    picked = jax.random.randint(key_pick, (DOCS,), 0, N_CTX - 1).astype(jnp.int32)
    signs = (jax.random.randint(key_sign, (DOCS,), 0, 2) * 2 - 1).astype(jnp.int32)
    column = jnp.arange(N_CTX - 1, dtype=jnp.int32)
    shifts = jnp.where(column[None, :] == picked[:, None], (signs * HW)[:, None], shifts)
    zero_col = jnp.zeros((DOCS, 1), jnp.int32)
    offsets = jnp.concatenate([zero_col, shifts, zero_col], axis=1)
    bounds = jnp.arange(N_CTX + 1, dtype=jnp.int32)[None, :] * TT + offsets
    extra = bounds[:, 1:] - bounds[:, :-1] - SS
    slot_keys = jax.random.split(key_slots, DOCS * N_CTX)
    orders = jax.vmap(lambda one_key: jax.random.permutation(one_key, SS * 3 - 3))(slot_keys)
    orders = orders.reshape(DOCS, N_CTX, SS * 3 - 3).astype(jnp.int32)
    front = jnp.full((DOCS, N_CTX, 3), SS * 3, jnp.int32)
    orders = jnp.concatenate([front, orders], axis=-1)
    chosen = (orders < extra[:, :, None]).astype(jnp.int32)
    lengths = 1 + jnp.sum(chosen.reshape(DOCS, N_CTX, SS, 3), axis=-1)
    span_ends = bounds[:, :-1, None] + jnp.cumsum(lengths, axis=-1)
    return span_ends.reshape(DOCS, SLEN).astype(jnp.int32)


def steps_of(rng, shape, shards, smallest, top_value):
    factor_of = 1.0
    for dim, shards_of in shards:
        steps = jax.random.uniform(jax.random.fold_in(jax.random.fold_in(rng, 6), dim), (shards_of,), jnp.float32, smallest / len(shards), top_value / len(shards))
        factor_of = factor_of * jnp.repeat(jnp.exp(steps), shape[dim] // shards_of).reshape((-1,) + (1,) * (len(shape) - 1 - dim))
    return factor_of


def noise(key, extent, deviation, most, cuts=(), held_as=jnp.bfloat16):
    level = steps_of(key, extent, cuts, -0.22, 0.18) if cuts else 1.0
    values = jax.random.normal(key, extent, jnp.float32) * deviation * level
    return jnp.minimum(jnp.maximum(values, -most), most).astype(held_as)


def setup_inputs(seed: int = 0, part: int = 0) -> dict:
    keys = jax.random.split(jax.random.key(seed), 5)
    part_splits = jax.random.split(jax.random.fold_in(keys[4], part), 5)
    return {
        "teacher_rows": noise(part_splits[0], (DOCS, TLEN, D), 1.0, 6.0, ((0, 2), (1, 4), (2, 2))),
        "student_hidden": noise(part_splits[1], (DOCS, SLEN, E), 1.0, 6.0, ((0, 2), (1, 4), (2, 2))),
        "projector": noise(keys[2], (D, E), D ** -0.5, 0.09375, ((1, 2),)),
        "span_end": draw_span_end(jax.random.fold_in(jax.random.fold_in(keys[4], part), 71), part),
    }


epsilon = 1e-06

def reference(teacher_rows, student_hidden, projector, span_end):
    losses = []
    w_grad = jnp.zeros((D, E), jnp.float32)
    positions = jnp.arange(TLEN, dtype=jnp.int32)
    for document in range(DOCS):
        span_ends = span_end[document]
        span_starts = jnp.concatenate([jnp.zeros((1,), jnp.int32), span_ends[:-1]])
        owner = jnp.searchsorted(span_ends, positions, side='right').astype(jnp.int32)
        sums = jax.ops.segment_sum(teacher_rows[document].astype(jnp.float32), owner, num_segments=SLEN)
        counts = (span_ends - span_starts).astype(jnp.float32)
        pooled = (sums / counts[:, None]).astype(jnp.bfloat16)
        projected = jnp.dot(pooled, projector, preferred_element_type=jnp.float32)
        hidden = student_hidden[document].astype(jnp.float32)
        inner = lax.optimization_barrier(jnp.sum(projected * hidden, axis=1))
        psq = lax.optimization_barrier(jnp.sum(projected * projected, axis=1))
        hsq = lax.optimization_barrier(jnp.sum(hidden * hidden, axis=1))
        scale = lax.rsqrt((psq + epsilon) * (hsq + epsilon))
        losses.append(1.0 - inner * scale)
        proj_grad = ((inner * scale / (psq + epsilon))[:, None] * projected - scale[:, None] * hidden).astype(jnp.bfloat16)
        w_grad = w_grad + lax.dot_general(pooled, proj_grad, (((0,), (0,)), ((), ())), preferred_element_type=jnp.float32)
    return (jnp.stack(losses), w_grad)
```

```python
import jax
import jax.numpy as jnp
from jax import lax
from jax.experimental import pallas as pl
from jax.experimental.pallas import tpu as pltpu
from jax.sharding import PartitionSpec as P

epsilon = 1e-06
MESH = pl.DeviceIdType.MESH
F32 = jnp.float32
BF16 = jnp.bfloat16


def remote(src, dst, send, recv, device):
    return pltpu.make_async_remote_copy(
        src_ref=src, dst_ref=dst, send_sem=send, recv_sem=recv,
        device_id=device, device_id_type=MESH,
    )


def kernel(
    teach, hid, weight, end_ref, loss_ref, out_ref,
    window, wbuf, hbuf, pool, other, proj, pg, pgo, sbuf, rbuf,
    start_col, end_col, stat, stat_in,
    loc_sem, halo_s, halo_r, mp_s, mp_r, x_s, x_r, f_s, f_r,
    st_s, st_r, pg_s, pg_r, z_s, z_r,
):
    rows, rim = teach.shape[0], teach.shape[0] // 8
    tokens = hid.shape[0]
    chunk = pool.shape[2]
    blocks, width = pg.shape[0], pg.shape[2]
    c, p, m = (lax.axis_index("ctx"), lax.axis_index("dp"), lax.axis_index("mp"))
    mate, twin = {"mp": 1 - m}, {"dp": 1 - p}
    mine, theirs = 4 * m, 4 * (1 - m)

    load_t = pltpu.make_async_copy(teach, window.at[pl.ds(rim, rows)], loc_sem.at[0])
    load_w = pltpu.make_async_copy(weight, wbuf, loc_sem.at[1])
    load_h = pltpu.make_async_copy(hid, hbuf, loc_sem.at[2])
    load_t.start()
    load_w.start()
    load_h.start()

    barrier = pltpu.get_barrier_semaphore()
    for step in (1, 2, 3):
        pl.semaphore_signal(
            barrier, inc=1, device_id={"ctx": lax.rem(c + step, 4)}, device_id_type=MESH
        )
    pl.semaphore_signal(barrier, inc=1, device_id=mate, device_id_type=MESH)
    pl.semaphore_signal(barrier, inc=1, device_id=twin, device_id_type=MESH)
    pl.semaphore_wait(barrier, 5)

    before = window.at[pl.ds(0, rim)]
    after = window.at[pl.ds(rim + rows, rim)]
    halo_up = remote(
        teach.at[pl.ds(rows - rim, rim)], before, halo_s.at[0], halo_r.at[0],
        {"ctx": lax.rem(c + 1, 4)},
    )
    halo_down = remote(
        teach.at[pl.ds(0, rim)], after, halo_s.at[1], halo_r.at[1],
        {"ctx": lax.rem(c + 3, 4)},
    )

    @pl.when(c < 3)
    def _():
        halo_up.start()

    @pl.when(c > 0)
    def _():
        halo_down.start()

    @pl.when(c == 0)
    def _():
        before[...] = jnp.zeros((rim, window.shape[1]), BF16)

    @pl.when(c == 3)
    def _():
        after[...] = jnp.zeros((rim, window.shape[1]), BF16)

    ends = jnp.broadcast_to(end_ref[...], (8, tokens)) - (c * rows - rim)
    lane = lax.broadcasted_iota(jnp.int32, (8, tokens), 1)
    starts = jnp.where(lane == 0, ends - 1, pltpu.roll(ends, 1, 1))
    for i in range(tokens // 128):
        at = slice(i * 128, i * 128 + 128)
        end_col[at, :] = jnp.broadcast_to(ends[0:1, at], (128, 128)).T
        start_col[at, :] = jnp.broadcast_to(starts[0:1, at], (128, 128)).T

    def pool_block(first, count, low, depth):
        at = pl.ds(first, count)
        begin, stop = start_col[at, 0:1], end_col[at, 0:1]
        place = low + lax.broadcasted_iota(jnp.int32, (count, depth), 1)
        member = jnp.where((place >= begin) & (place < stop), 1.0, 0.0).astype(BF16)
        share = 1.0 / (stop - begin).astype(F32)
        for q in range(4):
            sums = jnp.dot(
                member, window[pl.ds(low, depth), q * chunk:(q + 1) * chunk],
                preferred_element_type=F32,
            )
            pool[mine + q, at, :] = (sums * share).astype(BF16)

    pieces = ((rim, tokens - 2 * rim), (0, rim), (tokens - rim, rim))

    def mp_copy(i, slots):
        ref = pool.at[pl.ds(slots, 4), pl.ds(*pieces[i])]
        return remote(ref, ref, mp_s.at[i], mp_r.at[i], mate)

    def x_copy(i, k):
        return remote(
            pool.at[mine + 2 * k + 1 - p, pl.ds(*pieces[i])],
            other.at[2 * m + k, pl.ds(*pieces[i])],
            x_s.at[i, k], x_r.at[i, k], twin,
        )

    def f_copy(i, k, half):
        ref = other.at[2 * half + k, pl.ds(*pieces[i])]
        return remote(ref, ref, f_s.at[i, k], f_r.at[i, k], mate)

    def share_piece(i):
        mp_copy(i, mine).start()
        x_copy(i, 0).start()
        x_copy(i, 1).start()

    def project(first, count, base, fresh):
        at = pl.ds(first, count)
        total = jnp.dot(pool[base, at, :], wbuf[base], preferred_element_type=F32)
        for q in range(1, 4):
            total += jnp.dot(
                pool[base + q, at, :], wbuf[base + q], preferred_element_type=F32
            )
        proj[at, :] = total if fresh else proj[at, :] + total

    middle = tokens - 2 * rim
    half = middle // 2
    reach = rows - tokens + 2 * rim
    load_t.wait()
    for i in range(2):
        low = rim + i * half
        pool_block(low, half, low, half + reach)
    share_piece(0)
    load_w.wait()
    for i in range(2):
        project(rim + i * half, half, mine, True)

    @pl.when(c > 0)
    def _():
        halo_up.wait_recv()

    pool_block(0, rim, 0, rim + reach)
    share_piece(1)

    @pl.when(c < 3)
    def _():
        halo_down.wait_recv()

    pool_block(tokens - rim, rim, tokens - rim, rim + reach)
    share_piece(2)
    project(0, rim, mine, True)
    project(tokens - rim, rim, mine, True)
    mp_copy(0, theirs).wait_recv()
    for i in range(2):
        project(rim + i * half, half, theirs, False)
    mp_copy(1, theirs).wait_recv()
    project(0, rim, theirs, False)
    mp_copy(2, theirs).wait_recv()
    project(tokens - rim, rim, theirs, False)
    load_h.wait()

    place = lax.broadcasted_iota(jnp.int32, (128, 128), 1)
    for i in range(tokens // 128):
        at = slice(i * 128, i * 128 + 128)
        projected, hidden = proj[at, :], hbuf[at, :].astype(F32)
        inner = jnp.sum(projected * hidden, axis=1, keepdims=True)
        psq = jnp.sum(projected * projected, axis=1, keepdims=True)
        hsq = jnp.sum(hidden * hidden, axis=1, keepdims=True)
        packed = jnp.where(place == 0, inner, jnp.where(place == 1, psq, hsq))
        stat[:, at] = packed.T[0:8, :]
    swap = remote(stat, stat_in, st_s, st_r, mate)
    swap.start()
    swap.wait()
    total = stat[...] + stat_in[...]
    inner, psq, hsq = total[0:1], total[1:2], total[2:3]
    scale = lax.rsqrt((psq + epsilon) * (hsq + epsilon))
    loss_ref[...] = 1.0 - inner * scale
    ratio = inner * scale / (psq + epsilon)
    for i in range(tokens // 128):
        at = slice(i * 128, i * 128 + 128)
        a = jnp.broadcast_to(ratio[:, at], (128, 128)).T[:, 0:1]
        b = jnp.broadcast_to(scale[:, at], (128, 128)).T[:, 0:1]
        grad = (a * proj[at, :] - b * hbuf[at, :].astype(F32)).astype(BF16)
        for j in range(blocks):
            pg[j, at, :] = grad[:, j * width:(j + 1) * width]

    def pg_copy(j):
        return remote(pg.at[j], pgo.at[j], pg_s.at[j], pg_r.at[j], twin)

    for j in range(blocks):
        pg_copy(j).start()
    for i in range(3):
        for k in range(2):
            x_copy(i, k).wait_recv()
            f_copy(i, k, m).start()
    for i in range(3):
        for k in range(2):
            f_copy(i, k, 1 - m).wait_recv()

    upper = c // 2
    edge = c * (1 - upper) + (3 - c) * upper

    def mirrored(d):
        return d * (1 - upper) + (3 - d) * upper

    def partial(d, j):
        dims = (((0,), (0,)), ((), ()))
        return lax.dot_general(
            pool[2 * d + p], pg[j], dims, preferred_element_type=F32
        ) + lax.dot_general(other[d], pgo[j], dims, preferred_element_type=F32)

    routes = (
        (mirrored(3 - edge), mirrored(1 + edge), edge),
        (mirrored(2 - 2 * edge), mirrored(2 - 2 * edge), 2),
        (mirrored(1 + 2 * edge), mirrored(1 + 2 * edge), 3),
    )

    def z_copy(s, j):
        _, device, slot = routes[s]
        return remote(
            sbuf.at[s, j], rbuf.at[slot, j], z_s.at[s, j], z_r.at[slot, j],
            {"ctx": device},
        )

    def landed(slot, j):
        ref = rbuf.at[slot, j]
        remote(
            ref, ref, z_s.at[0, j], z_r.at[slot, j], {"ctx": lax.rem(c + 1, 4)}
        ).wait_recv()

    def send_block(j, carry):
        pg_copy(j).wait_recv()
        for s in range(2):
            sbuf[s, j] = partial(routes[s][0], j).astype(BF16)
            z_copy(s, j).start()
        value = partial(routes[2][0], j)

        @pl.when(edge == 0)
        def _():
            sbuf[2, j] = value.astype(BF16)

        @pl.when(edge == 1)
        def _():
            landed(0, j)
            sbuf[2, j] = (value + rbuf[0, j].astype(F32)).astype(BF16)

        z_copy(2, j).start()
        return carry

    lax.fori_loop(0, blocks, send_block, 0)
    for j in range(blocks):
        out_ref[:, j * width:(j + 1) * width] = partial(c, j)
    for j in range(blocks):
        at = slice(j * width, (j + 1) * width)

        @pl.when(edge == 1)
        def _():
            landed(1, j)
            out_ref[:, at] += rbuf[1, j].astype(F32)

        landed(2, j)
        landed(3, j)
        out_ref[:, at] += rbuf[2, j].astype(F32) + rbuf[3, j].astype(F32)

    @pl.when(c < 3)
    def _():
        halo_up.wait_send()

    @pl.when(c > 0)
    def _():
        halo_down.wait_send()

    for i in range(3):
        mp_copy(i, mine).wait_send()
        for k in range(2):
            x_copy(i, k).wait_send()
            f_copy(i, k, m).wait_send()
    for j in range(blocks):
        pg_copy(j).wait_send()
        for s in range(3):
            z_copy(s, j).wait_send()


def fused(teacher_rows, student_hidden, projector, span_end):
    rows, features = teacher_rows.shape[1:]
    tokens, columns = student_hidden.shape[1:]
    depth = 2 * features
    chunk, blocks = depth // 8, 3
    width, rim = columns // blocks, rows // 8
    anywhere = pl.BlockSpec(memory_space=pl.ANY)
    local = pl.BlockSpec(memory_space=pltpu.VMEM)
    dma = pltpu.SemaphoreType.DMA
    return tuple(pl.pallas_call(
        kernel,
        out_shape=(
            jax.ShapeDtypeStruct((1, tokens), F32),
            jax.ShapeDtypeStruct((chunk, columns), F32),
        ),
        in_specs=[anywhere, anywhere, anywhere, local],
        out_specs=(local, local),
        scratch_shapes=[
            pltpu.VMEM((rows + 2 * rim, features), BF16),
            pltpu.VMEM((8, chunk, columns), BF16),
            pltpu.VMEM((tokens, columns), BF16),
            pltpu.VMEM((8, tokens, chunk), BF16),
            pltpu.VMEM((4, tokens, chunk), BF16),
            pltpu.VMEM((tokens, columns), F32),
            pltpu.VMEM((blocks, tokens, width), BF16),
            pltpu.VMEM((blocks, tokens, width), BF16),
            pltpu.VMEM((3, blocks, chunk, width), BF16),
            pltpu.VMEM((4, blocks, chunk, width), BF16),
            pltpu.VMEM((tokens, 128), jnp.int32),
            pltpu.VMEM((tokens, 128), jnp.int32),
            pltpu.VMEM((8, tokens), F32),
            pltpu.VMEM((8, tokens), F32),
            dma((3,)), dma((2,)), dma((2,)), dma((3,)), dma((3,)),
            dma((3, 2)), dma((3, 2)), dma((3, 2)), dma((3, 2)),
            dma, dma, dma((blocks,)), dma((blocks,)),
            dma((3, blocks)), dma((4, blocks)),
        ],
        compiler_params=pltpu.CompilerParams(
            collective_id=0, has_side_effects=True, vmem_limit_bytes=56 * 1024 * 1024
        ),
        cost_estimate=pl.CostEstimate(
            flops=14_000_000_000, bytes_accessed=14_000_000, transcendentals=768
        ),
    )(
        teacher_rows[0], student_hidden[0],
        projector.reshape(8, chunk, columns), span_end,
    ))


def shifted(block, axis, distance):
    devices = range(lax.axis_size(axis))
    route = [(i - distance, i) for i in devices if i - distance in devices]
    return lax.ppermute(block, axis, route)


def extended(value, sides, width):
    for axis, dim in sides:
        size, length = (lax.axis_size(axis), value.shape[dim])
        up = [(i, (i + 1) % size) for i in range(size - 1)]
        down = [(j, i) for i, j in up]
        last = lax.slice_in_dim(value, length - width, length, axis=dim)
        first = lax.slice_in_dim(value, 0, width, axis=dim)
        before = lax.ppermute(last, axis, up)
        after = lax.ppermute(first, axis, down)
        value = jnp.concatenate([before, value, after], axis=dim)
    return value


def body(teacher_rows, student_hidden, projector, span_end):
    teacher = teacher_rows[0]
    span_ends = span_end[0]
    teach_rows = teacher.shape[0]
    rim_width = teach_rows // 8
    earlier = shifted(span_ends[-1:], "ctx", 1)
    span_starts = jnp.concatenate([earlier, span_ends[:-1]])
    window = extended(teacher, (("ctx", 0),), rim_width)
    window_start = lax.axis_index("ctx") * teach_rows - rim_width
    positions = window_start + jnp.arange(teach_rows + 2 * rim_width, dtype=jnp.int32)
    member = (positions[None, :] >= span_starts[:, None]) & (
        positions[None, :] < span_ends[:, None]
    )
    sums = jnp.dot(member.astype(jnp.bfloat16), window, preferred_element_type=jnp.float32)
    counts = (span_ends - span_starts).astype(jnp.float32)
    pooled_half = (sums / counts[:, None]).astype(jnp.bfloat16)
    pooled = lax.all_gather(pooled_half, "mp", axis=1, tiled=True)
    projected = jnp.dot(pooled, projector, preferred_element_type=jnp.float32)
    hidden = student_hidden[0].astype(jnp.float32)
    inner, psq, hsq = lax.psum(
        (
            jnp.sum(projected * hidden, axis=1),
            jnp.sum(projected * projected, axis=1),
            jnp.sum(hidden * hidden, axis=1),
        ),
        "mp",
    )
    scale = lax.rsqrt((psq + epsilon) * (hsq + epsilon))
    token_loss = (1.0 - inner * scale)[None, :]
    proj_grad = (
        (inner * scale / (psq + epsilon))[:, None] * projected - scale[:, None] * hidden
    ).astype(jnp.bfloat16)
    w_grad = lax.psum_scatter(
        lax.dot_general(
            pooled, proj_grad, (((0,), (0,)), ((), ())), preferred_element_type=jnp.float32
        ),
        ("ctx", "dp"),
        scatter_dimension=0,
        tiled=True,
    )
    return (token_loss, w_grad)


def solution(mesh):
    sizes = tuple(mesh.shape[axis] for axis in ("ctx", "dp", "mp"))
    return jax.shard_map(
        fused if sizes == (4, 2, 2) else body,
        mesh=mesh,
        in_specs=(
            P("dp", ("groups", "ctx"), "mp"),
            P("dp", ("groups", "ctx"), "mp"),
            P(None, "mp"),
            P("dp", ("groups", "ctx")),
        ),
        out_specs=(P("dp", ("groups", "ctx")), P(("groups", "ctx", "dp"), "mp")),
        check_vma=False,
    )
```

```python
import jax
import jax.numpy as jnp
from jax import lax
from jax.experimental import pallas as pl
from jax.experimental.pallas import tpu as pltpu
from jax.sharding import PartitionSpec as P

epsilon = 1e-06
MESH = pl.DeviceIdType.MESH
F32 = jnp.float32
BF16 = jnp.bfloat16


def remote(src, dst, send, recv, device):
    return pltpu.make_async_remote_copy(
        src_ref=src, dst_ref=dst, send_sem=send, recv_sem=recv,
        device_id=device, device_id_type=MESH,
    )


def kernel(
    teach, hid, weight, end_ref, loss_ref, out_ref,
    window, wbuf, hbuf, pool, other, proj, pg, pgo, sbuf, rbuf,
    start_col, end_col, stat, stat_in,
    loc_sem, halo_s, halo_r, mp_s, mp_r, x_s, x_r, f_s, f_r,
    st_s, st_r, pg_s, pg_r, z_s, z_r,
):
    rows, rim = teach.shape[0], teach.shape[0] // 8
    tokens = hid.shape[0]
    chunk = pool.shape[2]
    blocks, width = pg.shape[0], pg.shape[2]
    c, p, m = (lax.axis_index("ctx"), lax.axis_index("dp"), lax.axis_index("mp"))
    mate, twin = {"mp": 1 - m}, {"dp": 1 - p}
    mine, theirs = 4 * m, 4 * (1 - m)

    load_t = pltpu.make_async_copy(teach, window.at[pl.ds(rim, rows)], loc_sem.at[0])
    load_w = pltpu.make_async_copy(weight, wbuf, loc_sem.at[1])
    load_h = pltpu.make_async_copy(hid, hbuf, loc_sem.at[2])
    load_t.start()
    load_w.start()
    load_h.start()

    barrier = pltpu.get_barrier_semaphore()
    for step in (1, 2, 3):
        pl.semaphore_signal(
            barrier, inc=1, device_id={"ctx": lax.rem(c + step, 4)}, device_id_type=MESH
        )
    pl.semaphore_signal(barrier, inc=1, device_id=mate, device_id_type=MESH)
    pl.semaphore_signal(barrier, inc=1, device_id=twin, device_id_type=MESH)
    pl.semaphore_wait(barrier, 5)

    before = window.at[pl.ds(0, rim)]
    after = window.at[pl.ds(rim + rows, rim)]
    halo_up = remote(
        teach.at[pl.ds(rows - rim, rim)], before, halo_s.at[0], halo_r.at[0],
        {"ctx": lax.rem(c + 1, 4)},
    )
    halo_down = remote(
        teach.at[pl.ds(0, rim)], after, halo_s.at[1], halo_r.at[1],
        {"ctx": lax.rem(c + 3, 4)},
    )

    @pl.when(c < 3)
    def _():
        halo_up.start()

    @pl.when(c > 0)
    def _():
        halo_down.start()

    @pl.when(c == 0)
    def _():
        before[...] = jnp.zeros((rim, window.shape[1]), BF16)

    @pl.when(c == 3)
    def _():
        after[...] = jnp.zeros((rim, window.shape[1]), BF16)

    ends = jnp.broadcast_to(end_ref[...], (8, tokens)) - (c * rows - rim)
    lane = lax.broadcasted_iota(jnp.int32, (8, tokens), 1)
    starts = jnp.where(lane == 0, ends - 1, pltpu.roll(ends, 1, 1))
    for i in range(tokens // 128):
        at = slice(i * 128, i * 128 + 128)
        end_col[at, :] = jnp.broadcast_to(ends[0:1, at], (128, 128)).T
        start_col[at, :] = jnp.broadcast_to(starts[0:1, at], (128, 128)).T

    def pool_block(top, count, low, depth):
        at = pl.ds(top, count)
        begin, stop = start_col[at, 0:1], end_col[at, 0:1]
        place = low + lax.broadcasted_iota(jnp.int32, (count, depth), 1)
        member = jnp.where((place >= begin) & (place < stop), 1.0, 0.0).astype(BF16)
        share = 1.0 / (stop - begin).astype(F32)
        for q in range(4):
            sums = jnp.dot(
                member, window[pl.ds(low, depth), q * chunk:(q + 1) * chunk],
                preferred_element_type=F32,
            )
            pool[mine + q, at, :] = (sums * share).astype(BF16)

    first, second = 1 - lax.rem(c, 2), lax.rem(c, 2)
    upper = c // 2
    edge = c * (1 - upper) + (3 - c) * upper
    near = m + upper == 1
    pieces = ((rim, tokens - 2 * rim), (0, rim), (tokens - rim, rim))

    def mp_copy(i, slots):
        ref = pool.at[pl.ds(slots, 4), pl.ds(*pieces[i])]
        return remote(ref, ref, mp_s.at[i], mp_r.at[i], mate)

    def x_copy(i, turn, k):
        return remote(
            pool.at[mine + 2 * k + 1 - p, pl.ds(*pieces[i])],
            other.at[2 * m + k, pl.ds(*pieces[i])],
            x_s.at[i, turn], x_r.at[i, turn], twin,
        )

    def f_copy(i, turn, k, owner):
        ref = other.at[2 * owner + k, pl.ds(*pieces[i])]
        return remote(ref, ref, f_s.at[i, turn], f_r.at[i, turn], mate)

    def x_start(turn, k):
        for i in range(3):
            x_copy(i, turn, k).start()

    def forward(turn, k):
        for i in range(3):
            x_copy(i, turn, k).wait_recv()
            f_copy(i, turn, k, m).start()

    def forwarded(turn, k):
        for i in range(3):
            f_copy(i, turn, k, 1 - m).wait_recv()

    def share_piece(i):
        mp_copy(i, mine).start()

        @pl.when((edge == 1) | near)
        def _():
            x_copy(i, 0, first).start()

        @pl.when((edge == 0) & near)
        def _():
            x_copy(i, 1, second).start()

    def project(top, count, base, fresh):
        at = pl.ds(top, count)
        total = jnp.dot(pool[base, at, :], wbuf[base], preferred_element_type=F32)
        for q in range(1, 4):
            total += jnp.dot(
                pool[base + q, at, :], wbuf[base + q], preferred_element_type=F32
            )
        proj[at, :] = total if fresh else proj[at, :] + total

    middle = tokens - 2 * rim
    half = middle // 2
    reach = rows - tokens + 2 * rim
    load_t.wait()
    for i in range(2):
        low = rim + i * half
        pool_block(low, half, low, half + reach)
    share_piece(0)
    load_w.wait()
    for i in range(2):
        project(rim + i * half, half, mine, True)

    @pl.when(c > 0)
    def _():
        halo_up.wait_recv()

    pool_block(0, rim, 0, rim + reach)
    share_piece(1)

    @pl.when(c < 3)
    def _():
        halo_down.wait_recv()

    pool_block(tokens - rim, rim, tokens - rim, rim + reach)
    share_piece(2)
    project(0, rim, mine, True)
    project(tokens - rim, rim, mine, True)
    mp_copy(0, theirs).wait_recv()
    for i in range(2):
        project(rim + i * half, half, theirs, False)
    mp_copy(1, theirs).wait_recv()
    project(0, rim, theirs, False)
    mp_copy(2, theirs).wait_recv()
    project(tokens - rim, rim, theirs, False)
    load_h.wait()

    place = lax.broadcasted_iota(jnp.int32, (128, 128), 1)
    for i in range(tokens // 128):
        at = slice(i * 128, i * 128 + 128)
        projected, hidden = proj[at, :], hbuf[at, :].astype(F32)
        inner = jnp.sum(projected * hidden, axis=1, keepdims=True)
        psq = jnp.sum(projected * projected, axis=1, keepdims=True)
        hsq = jnp.sum(hidden * hidden, axis=1, keepdims=True)
        packed = jnp.where(place == 0, inner, jnp.where(place == 1, psq, hsq))
        stat[:, at] = packed.T[0:8, :]
    swap = remote(stat, stat_in, st_s, st_r, mate)
    swap.start()
    swap.wait()
    total = stat[...] + stat_in[...]
    inner, psq, hsq = total[0:1], total[1:2], total[2:3]
    scale = lax.rsqrt((psq + epsilon) * (hsq + epsilon))
    loss_ref[...] = 1.0 - inner * scale
    ratio = inner * scale / (psq + epsilon)
    for i in range(tokens // 128):
        at = slice(i * 128, i * 128 + 128)
        a = jnp.broadcast_to(ratio[:, at], (128, 128)).T[:, 0:1]
        b = jnp.broadcast_to(scale[:, at], (128, 128)).T[:, 0:1]
        grad = (a * proj[at, :] - b * hbuf[at, :].astype(F32)).astype(BF16)
        for j in range(blocks):
            pg[j, at, :] = grad[:, j * width:(j + 1) * width]

    def pg_copy(j):
        return remote(pg.at[j], pgo.at[j], pg_s.at[j], pg_r.at[j], twin)

    pg_copy(0).start()

    @pl.when(edge == 1)
    def _():
        forward(0, first)
        forwarded(0, first)

    @pl.when((edge == 0) & near)
    def _():
        forward(0, first)
        forward(1, second)

    @pl.when((edge == 0) & (m + upper != 1))
    def _():
        forwarded(0, first)
        forwarded(1, second)

    def mirrored(d):
        return d * (1 - upper) + (3 - d) * upper

    def partial(d, j):
        dims = (((0,), (0,)), ((), ()))
        return lax.dot_general(
            pool[2 * d + p], pg[j], dims, preferred_element_type=F32
        ) + lax.dot_general(other[d], pgo[j], dims, preferred_element_type=F32)

    routes = (
        (mirrored(3 - edge), mirrored(1 + edge), edge),
        (mirrored(2 - 2 * edge), mirrored(2 - 2 * edge), 2),
        (mirrored(1 + 2 * edge), mirrored(1 + 2 * edge), 3),
    )

    def z_copy(s, j):
        _, device, slot = routes[s]
        return remote(
            sbuf.at[s, j], rbuf.at[slot, j], z_s.at[s, j], z_r.at[slot, j],
            {"ctx": device},
        )

    def landed(slot, j):
        ref = rbuf.at[slot, j]
        remote(
            ref, ref, z_s.at[0, j], z_r.at[slot, j], {"ctx": lax.rem(c + 1, 4)}
        ).wait_recv()

    def send_block(j, carry):
        pg_copy(j).wait()

        @pl.when(j + 1 < blocks)
        def _():
            pg_copy(j + 1).start()

        for s in range(2):
            sbuf[s, j] = partial(routes[s][0], j).astype(BF16)
            z_copy(s, j).start()
        return carry

    def send_last(j, carry):
        value = partial(routes[2][0], j)

        @pl.when(edge == 0)
        def _():
            sbuf[2, j] = value.astype(BF16)

        @pl.when(edge == 1)
        def _():
            landed(0, j)
            sbuf[2, j] = (value + rbuf[0, j].astype(F32)).astype(BF16)

        z_copy(2, j).start()
        return carry

    lax.fori_loop(0, blocks, send_block, 0)

    far = m + upper != 1

    @pl.when((edge == 1) & near)
    def _():
        x_start(1, second)
        forward(1, second)

    @pl.when((edge == 1) & far)
    def _():
        forwarded(1, second)
        x_start(1, second)

    @pl.when((edge == 0) & near)
    def _():
        forwarded(0, first)

    @pl.when((edge == 0) & far)
    def _():
        x_start(0, first)
        forward(0, first)
        x_start(1, second)

    lax.fori_loop(0, blocks, send_last, 0)

    @pl.when(near)
    def _():
        forwarded(1, second)

    @pl.when(far)
    def _():
        forward(1, second)

    for j in range(blocks):
        out_ref[:, j * width:(j + 1) * width] = partial(c, j)
    for j in range(blocks):
        at = slice(j * width, (j + 1) * width)

        @pl.when(edge == 1)
        def _():
            landed(1, j)
            out_ref[:, at] += rbuf[1, j].astype(F32)

        landed(2, j)
        landed(3, j)
        out_ref[:, at] += rbuf[2, j].astype(F32) + rbuf[3, j].astype(F32)

    @pl.when(c < 3)
    def _():
        halo_up.wait_send()

    @pl.when(c > 0)
    def _():
        halo_down.wait_send()

    for i in range(3):
        mp_copy(i, mine).wait_send()
        for turn, k in ((0, first), (1, second)):
            x_copy(i, turn, k).wait_send()
            f_copy(i, turn, k, m).wait_send()
    for j in range(blocks):
        for s in range(3):
            z_copy(s, j).wait_send()


def fused(teacher_rows, student_hidden, projector, span_end):
    rows, features = teacher_rows.shape[1:]
    tokens, columns = student_hidden.shape[1:]
    depth = 2 * features
    chunk, blocks = depth // 8, 3
    width, rim = columns // blocks, rows // 8
    anywhere = pl.BlockSpec(memory_space=pl.ANY)
    local = pl.BlockSpec(memory_space=pltpu.VMEM)
    dma = pltpu.SemaphoreType.DMA
    return tuple(pl.pallas_call(
        kernel,
        out_shape=(
            jax.ShapeDtypeStruct((1, tokens), F32),
            jax.ShapeDtypeStruct((chunk, columns), F32),
        ),
        in_specs=[anywhere, anywhere, anywhere, local],
        out_specs=(local, local),
        scratch_shapes=[
            pltpu.VMEM((rows + 2 * rim, features), BF16),
            pltpu.VMEM((8, chunk, columns), BF16),
            pltpu.VMEM((tokens, columns), BF16),
            pltpu.VMEM((8, tokens, chunk), BF16),
            pltpu.VMEM((4, tokens, chunk), BF16),
            pltpu.VMEM((tokens, columns), F32),
            pltpu.VMEM((blocks, tokens, width), BF16),
            pltpu.VMEM((blocks, tokens, width), BF16),
            pltpu.VMEM((3, blocks, chunk, width), BF16),
            pltpu.VMEM((4, blocks, chunk, width), BF16),
            pltpu.VMEM((tokens, 128), jnp.int32),
            pltpu.VMEM((tokens, 128), jnp.int32),
            pltpu.VMEM((8, tokens), F32),
            pltpu.VMEM((8, tokens), F32),
            dma((3,)), dma((2,)), dma((2,)), dma((3,)), dma((3,)),
            dma((3, 2)), dma((3, 2)), dma((3, 2)), dma((3, 2)),
            dma, dma, dma((blocks,)), dma((blocks,)),
            dma((3, blocks)), dma((4, blocks)),
        ],
        compiler_params=pltpu.CompilerParams(
            collective_id=0, has_side_effects=True, vmem_limit_bytes=56 * 1024 * 1024
        ),
        cost_estimate=pl.CostEstimate(
            flops=14_000_000_000, bytes_accessed=14_000_000, transcendentals=768
        ),
    )(
        teacher_rows[0], student_hidden[0],
        projector.reshape(8, chunk, columns), span_end,
    ))


def shifted(block, axis, distance):
    devices = range(lax.axis_size(axis))
    route = [(i - distance, i) for i in devices if i - distance in devices]
    return lax.ppermute(block, axis, route)


def extended(value, sides, width):
    for axis, dim in sides:
        size, length = (lax.axis_size(axis), value.shape[dim])
        up = [(i, (i + 1) % size) for i in range(size - 1)]
        down = [(j, i) for i, j in up]
        last = lax.slice_in_dim(value, length - width, length, axis=dim)
        first = lax.slice_in_dim(value, 0, width, axis=dim)
        before = lax.ppermute(last, axis, up)
        after = lax.ppermute(first, axis, down)
        value = jnp.concatenate([before, value, after], axis=dim)
    return value


def body(teacher_rows, student_hidden, projector, span_end):
    teacher = teacher_rows[0]
    span_ends = span_end[0]
    teach_rows = teacher.shape[0]
    rim_width = teach_rows // 8
    earlier = shifted(span_ends[-1:], "ctx", 1)
    span_starts = jnp.concatenate([earlier, span_ends[:-1]])
    window = extended(teacher, (("ctx", 0),), rim_width)
    window_start = lax.axis_index("ctx") * teach_rows - rim_width
    positions = window_start + jnp.arange(teach_rows + 2 * rim_width, dtype=jnp.int32)
    member = (positions[None, :] >= span_starts[:, None]) & (
        positions[None, :] < span_ends[:, None]
    )
    sums = jnp.dot(member.astype(jnp.bfloat16), window, preferred_element_type=jnp.float32)
    counts = (span_ends - span_starts).astype(jnp.float32)
    pooled_half = (sums / counts[:, None]).astype(jnp.bfloat16)
    pooled = lax.all_gather(pooled_half, "mp", axis=1, tiled=True)
    projected = jnp.dot(pooled, projector, preferred_element_type=jnp.float32)
    hidden = student_hidden[0].astype(jnp.float32)
    inner, psq, hsq = lax.psum(
        (
            jnp.sum(projected * hidden, axis=1),
            jnp.sum(projected * projected, axis=1),
            jnp.sum(hidden * hidden, axis=1),
        ),
        "mp",
    )
    scale = lax.rsqrt((psq + epsilon) * (hsq + epsilon))
    token_loss = (1.0 - inner * scale)[None, :]
    proj_grad = (
        (inner * scale / (psq + epsilon))[:, None] * projected - scale[:, None] * hidden
    ).astype(jnp.bfloat16)
    w_grad = lax.psum_scatter(
        lax.dot_general(
            pooled, proj_grad, (((0,), (0,)), ((), ())), preferred_element_type=jnp.float32
        ),
        ("ctx", "dp"),
        scatter_dimension=0,
        tiled=True,
    )
    return (token_loss, w_grad)


def solution(mesh):
    sizes = tuple(mesh.shape[axis] for axis in ("ctx", "dp", "mp"))
    return jax.shard_map(
        fused if sizes == (4, 2, 2) else body,
        mesh=mesh,
        in_specs=(
            P("dp", ("groups", "ctx"), "mp"),
            P("dp", ("groups", "ctx"), "mp"),
            P(None, "mp"),
            P("dp", ("groups", "ctx")),
        ),
        out_specs=(P("dp", ("groups", "ctx")), P(("groups", "ctx", "dp"), "mp")),
        check_vma=False,
    )
```

```python
import jax
import jax.numpy as jnp
from jax import lax
from jax.experimental import pallas as pl
from jax.experimental.pallas import tpu as pltpu
from jax.sharding import PartitionSpec as P

epsilon = 1e-06
MESH = pl.DeviceIdType.MESH
F32 = jnp.float32
BF16 = jnp.bfloat16


def remote(src, dst, send, recv, device):
    return pltpu.make_async_remote_copy(
        src_ref=src, dst_ref=dst, send_sem=send, recv_sem=recv,
        device_id=device, device_id_type=MESH,
    )


def kernel(
    teach, hid, weight, end_ref, loss_ref, out_ref,
    window, wbuf, hbuf, pool, other, proj, pg, pgo, sbuf, rbuf,
    start_col, end_col, stat, stat_in,
    loc_sem, halo_s, halo_r, mp_s, mp_r, x_s, x_r, f_s, f_r,
    st_s, st_r, pg_s, pg_r, z_s, z_r,
):
    rows, rim = teach.shape[0], teach.shape[0] // 8
    tokens = hid.shape[0]
    chunk = pool.shape[2]
    blocks, width = pg.shape[0], pg.shape[2]
    c, p, m = (lax.axis_index("ctx"), lax.axis_index("dp"), lax.axis_index("mp"))
    mate, twin = {"mp": 1 - m}, {"dp": 1 - p}
    mine, theirs = 4 * m, 4 * (1 - m)

    load_t = pltpu.make_async_copy(teach, window.at[pl.ds(rim, rows)], loc_sem.at[0])
    load_w = pltpu.make_async_copy(weight, wbuf, loc_sem.at[1])
    load_h = pltpu.make_async_copy(hid, hbuf, loc_sem.at[2])
    load_t.start()
    load_w.start()
    load_h.start()

    barrier = pltpu.get_barrier_semaphore()
    for step in (1, 2, 3):
        pl.semaphore_signal(
            barrier, inc=1, device_id={"ctx": lax.rem(c + step, 4)}, device_id_type=MESH
        )
    pl.semaphore_signal(barrier, inc=1, device_id=mate, device_id_type=MESH)
    pl.semaphore_signal(barrier, inc=1, device_id=twin, device_id_type=MESH)
    pl.semaphore_wait(barrier, 5)

    before = window.at[pl.ds(0, rim)]
    after = window.at[pl.ds(rim + rows, rim)]
    halo_up = remote(
        teach.at[pl.ds(rows - rim, rim)], before, halo_s.at[0], halo_r.at[0],
        {"ctx": lax.rem(c + 1, 4)},
    )
    halo_down = remote(
        teach.at[pl.ds(0, rim)], after, halo_s.at[1], halo_r.at[1],
        {"ctx": lax.rem(c + 3, 4)},
    )

    @pl.when(c < 3)
    def _():
        halo_up.start()

    @pl.when(c > 0)
    def _():
        halo_down.start()

    @pl.when(c == 0)
    def _():
        before[...] = jnp.zeros((rim, window.shape[1]), BF16)

    @pl.when(c == 3)
    def _():
        after[...] = jnp.zeros((rim, window.shape[1]), BF16)

    ends = jnp.broadcast_to(end_ref[...], (8, tokens)) - (c * rows - rim)
    lane = lax.broadcasted_iota(jnp.int32, (8, tokens), 1)
    starts = jnp.where(lane == 0, ends - 1, pltpu.roll(ends, 1, 1))
    for i in range(tokens // 128):
        at = slice(i * 128, i * 128 + 128)
        end_col[at, :] = jnp.broadcast_to(ends[0:1, at], (128, 128)).T
        start_col[at, :] = jnp.broadcast_to(starts[0:1, at], (128, 128)).T

    def pool_block(top, count, low, depth):
        at = pl.ds(top, count)
        begin, stop = start_col[at, 0:1], end_col[at, 0:1]
        place = low + lax.broadcasted_iota(jnp.int32, (count, depth), 1)
        member = jnp.where((place >= begin) & (place < stop), 1.0, 0.0).astype(BF16)
        share = 1.0 / (stop - begin).astype(F32)
        for q in range(4):
            sums = jnp.dot(
                member, window[pl.ds(low, depth), q * chunk:(q + 1) * chunk],
                preferred_element_type=F32,
            )
            pool[mine + q, at, :] = (sums * share).astype(BF16)

    first, second = 1 - lax.rem(c, 2), lax.rem(c, 2)
    upper = c // 2
    edge = c * (1 - upper) + (3 - c) * upper
    near = m + upper == 1
    pieces = ((rim, tokens - 2 * rim), (0, rim), (tokens - rim, rim))

    def mp_copy(i, slots):
        ref = pool.at[pl.ds(slots, 4), pl.ds(*pieces[i])]
        return remote(ref, ref, mp_s.at[i], mp_r.at[i], mate)

    def x_copy(i, turn, k):
        return remote(
            pool.at[mine + 2 * k + 1 - p, pl.ds(*pieces[i])],
            other.at[2 * m + k, pl.ds(*pieces[i])],
            x_s.at[i, turn], x_r.at[i, turn], twin,
        )

    def f_copy(i, turn, k, owner):
        ref = other.at[2 * owner + k, pl.ds(*pieces[i])]
        return remote(ref, ref, f_s.at[i, turn], f_r.at[i, turn], mate)

    def x_start(turn, k):
        for i in range(3):
            x_copy(i, turn, k).start()

    def forward(turn, k):
        for i in range(3):
            x_copy(i, turn, k).wait_recv()
            f_copy(i, turn, k, m).start()

    def forwarded(turn, k):
        for i in range(3):
            f_copy(i, turn, k, 1 - m).wait_recv()

    def share_piece(i):
        mp_copy(i, mine).start()

        @pl.when((edge == 1) | near)
        def _():
            x_copy(i, 0, first).start()

        @pl.when((edge == 0) & near)
        def _():
            x_copy(i, 1, second).start()

    def project(top, count, base, fresh):
        at = pl.ds(top, count)
        total = jnp.dot(pool[base, at, :], wbuf[base], preferred_element_type=F32)
        for q in range(1, 4):
            total += jnp.dot(
                pool[base + q, at, :], wbuf[base + q], preferred_element_type=F32
            )
        proj[at, :] = total if fresh else proj[at, :] + total

    middle = tokens - 2 * rim
    half = middle // 2
    reach = rows - tokens + 2 * rim
    load_t.wait()
    for i in range(2):
        low = rim + i * half
        pool_block(low, half, low, half + reach)
    share_piece(0)
    load_w.wait()
    for i in range(2):
        project(rim + i * half, half, mine, True)
    mp_copy(0, theirs).wait_recv()
    for i in range(2):
        project(rim + i * half, half, theirs, False)

    @pl.when(c > 0)
    def _():
        halo_up.wait_recv()

    pool_block(0, rim, 0, rim + reach)
    share_piece(1)

    @pl.when(c < 3)
    def _():
        halo_down.wait_recv()

    pool_block(tokens - rim, rim, tokens - rim, rim + reach)
    share_piece(2)
    project(0, rim, mine, True)
    project(tokens - rim, rim, mine, True)
    mp_copy(1, theirs).wait_recv()
    project(0, rim, theirs, False)
    mp_copy(2, theirs).wait_recv()
    project(tokens - rim, rim, theirs, False)
    load_h.wait()

    place = lax.broadcasted_iota(jnp.int32, (128, 128), 1)
    for i in range(tokens // 128):
        at = slice(i * 128, i * 128 + 128)
        projected, hidden = proj[at, :], hbuf[at, :].astype(F32)
        inner = jnp.sum(projected * hidden, axis=1, keepdims=True)
        psq = jnp.sum(projected * projected, axis=1, keepdims=True)
        hsq = jnp.sum(hidden * hidden, axis=1, keepdims=True)
        packed = jnp.where(place == 0, inner, jnp.where(place == 1, psq, hsq))
        stat[:, at] = packed.T[0:8, :]
    swap = remote(stat, stat_in, st_s, st_r, mate)
    swap.start()
    swap.wait()
    total = stat[...] + stat_in[...]
    inner, psq, hsq = total[0:1], total[1:2], total[2:3]
    scale = lax.rsqrt((psq + epsilon) * (hsq + epsilon))
    loss_ref[...] = 1.0 - inner * scale
    ratio = inner * scale / (psq + epsilon)
    for i in range(tokens // 128):
        at = slice(i * 128, i * 128 + 128)
        a = jnp.broadcast_to(ratio[:, at], (128, 128)).T[:, 0:1]
        b = jnp.broadcast_to(scale[:, at], (128, 128)).T[:, 0:1]
        grad = (a * proj[at, :] - b * hbuf[at, :].astype(F32)).astype(BF16)
        for j in range(blocks):
            pg[j, at, :] = grad[:, j * width:(j + 1) * width]

    def pg_copy(j):
        return remote(pg.at[j], pgo.at[j], pg_s.at[j], pg_r.at[j], twin)

    pg_copy(0).start()

    @pl.when(edge == 1)
    def _():
        forward(0, first)
        forwarded(0, first)

    @pl.when((edge == 0) & near)
    def _():
        forward(0, first)
        forward(1, second)

    @pl.when((edge == 0) & (m + upper != 1))
    def _():
        forwarded(0, first)
        forwarded(1, second)

    def mirrored(d):
        return d * (1 - upper) + (3 - d) * upper

    def partial(d, j):
        dims = (((0,), (0,)), ((), ()))
        return lax.dot_general(
            pool[2 * d + p], pg[j], dims, preferred_element_type=F32
        ) + lax.dot_general(other[d], pgo[j], dims, preferred_element_type=F32)

    routes = (
        (mirrored(3 - edge), mirrored(1 + edge), edge),
        (mirrored(2 - 2 * edge), mirrored(2 - 2 * edge), 2),
        (mirrored(1 + 2 * edge), mirrored(1 + 2 * edge), 3),
    )

    def z_copy(s, j):
        _, device, slot = routes[s]
        return remote(
            sbuf.at[s, j], rbuf.at[slot, j], z_s.at[s, j], z_r.at[slot, j],
            {"ctx": device},
        )

    def landed(slot, j):
        ref = rbuf.at[slot, j]
        remote(
            ref, ref, z_s.at[0, j], z_r.at[slot, j], {"ctx": lax.rem(c + 1, 4)}
        ).wait_recv()

    def send_block(j, carry):
        pg_copy(j).wait()

        @pl.when(j + 1 < blocks)
        def _():
            pg_copy(j + 1).start()

        for s in range(2):
            sbuf[s, j] = partial(routes[s][0], j).astype(BF16)
            z_copy(s, j).start()
        return carry

    def send_last(j, carry):
        value = partial(routes[2][0], j)

        @pl.when(edge == 0)
        def _():
            sbuf[2, j] = value.astype(BF16)

        @pl.when(edge == 1)
        def _():
            landed(0, j)
            sbuf[2, j] = (value + rbuf[0, j].astype(F32)).astype(BF16)

        z_copy(2, j).start()
        return carry

    lax.fori_loop(0, blocks, send_block, 0)

    far = m + upper != 1

    @pl.when((edge == 1) & near)
    def _():
        x_start(1, second)
        forward(1, second)

    @pl.when((edge == 1) & far)
    def _():
        forwarded(1, second)
        x_start(1, second)

    @pl.when((edge == 0) & near)
    def _():
        forwarded(0, first)

    @pl.when((edge == 0) & far)
    def _():
        x_start(0, first)
        forward(0, first)
        x_start(1, second)

    lax.fori_loop(0, blocks, send_last, 0)

    @pl.when(near)
    def _():
        forwarded(1, second)

    @pl.when(far)
    def _():
        forward(1, second)

    for j in range(blocks):
        out_ref[:, j * width:(j + 1) * width] = partial(c, j)
    for j in range(blocks):
        at = slice(j * width, (j + 1) * width)

        @pl.when(edge == 1)
        def _():
            landed(1, j)
            out_ref[:, at] += rbuf[1, j].astype(F32)

        landed(2, j)
        landed(3, j)
        out_ref[:, at] += rbuf[2, j].astype(F32) + rbuf[3, j].astype(F32)

    @pl.when(c < 3)
    def _():
        halo_up.wait_send()

    @pl.when(c > 0)
    def _():
        halo_down.wait_send()

    for i in range(3):
        mp_copy(i, mine).wait_send()
        for turn, k in ((0, first), (1, second)):
            x_copy(i, turn, k).wait_send()
            f_copy(i, turn, k, m).wait_send()
    for j in range(blocks):
        for s in range(3):
            z_copy(s, j).wait_send()


def fused(teacher_rows, student_hidden, projector, span_end):
    rows, features = teacher_rows.shape[1:]
    tokens, columns = student_hidden.shape[1:]
    depth = 2 * features
    chunk, blocks = depth // 8, 3
    width, rim = columns // blocks, rows // 8
    anywhere = pl.BlockSpec(memory_space=pl.ANY)
    local = pl.BlockSpec(memory_space=pltpu.VMEM)
    dma = pltpu.SemaphoreType.DMA
    return tuple(pl.pallas_call(
        kernel,
        out_shape=(
            jax.ShapeDtypeStruct((1, tokens), F32),
            jax.ShapeDtypeStruct((chunk, columns), F32),
        ),
        in_specs=[anywhere, anywhere, anywhere, local],
        out_specs=(local, local),
        scratch_shapes=[
            pltpu.VMEM((rows + 2 * rim, features), BF16),
            pltpu.VMEM((8, chunk, columns), BF16),
            pltpu.VMEM((tokens, columns), BF16),
            pltpu.VMEM((8, tokens, chunk), BF16),
            pltpu.VMEM((4, tokens, chunk), BF16),
            pltpu.VMEM((tokens, columns), F32),
            pltpu.VMEM((blocks, tokens, width), BF16),
            pltpu.VMEM((blocks, tokens, width), BF16),
            pltpu.VMEM((3, blocks, chunk, width), BF16),
            pltpu.VMEM((4, blocks, chunk, width), BF16),
            pltpu.VMEM((tokens, 128), jnp.int32),
            pltpu.VMEM((tokens, 128), jnp.int32),
            pltpu.VMEM((8, tokens), F32),
            pltpu.VMEM((8, tokens), F32),
            dma((3,)), dma((2,)), dma((2,)), dma((3,)), dma((3,)),
            dma((3, 2)), dma((3, 2)), dma((3, 2)), dma((3, 2)),
            dma, dma, dma((blocks,)), dma((blocks,)),
            dma((3, blocks)), dma((4, blocks)),
        ],
        compiler_params=pltpu.CompilerParams(
            collective_id=0, has_side_effects=True, vmem_limit_bytes=56 * 1024 * 1024
        ),
        cost_estimate=pl.CostEstimate(
            flops=14_000_000_000, bytes_accessed=14_000_000, transcendentals=768
        ),
    )(
        teacher_rows[0], student_hidden[0],
        projector.reshape(8, chunk, columns), span_end,
    ))


def shifted(block, axis, distance):
    devices = range(lax.axis_size(axis))
    route = [(i - distance, i) for i in devices if i - distance in devices]
    return lax.ppermute(block, axis, route)


def extended(value, sides, width):
    for axis, dim in sides:
        size, length = (lax.axis_size(axis), value.shape[dim])
        up = [(i, (i + 1) % size) for i in range(size - 1)]
        down = [(j, i) for i, j in up]
        last = lax.slice_in_dim(value, length - width, length, axis=dim)
        first = lax.slice_in_dim(value, 0, width, axis=dim)
        before = lax.ppermute(last, axis, up)
        after = lax.ppermute(first, axis, down)
        value = jnp.concatenate([before, value, after], axis=dim)
    return value


def body(teacher_rows, student_hidden, projector, span_end):
    teacher = teacher_rows[0]
    span_ends = span_end[0]
    teach_rows = teacher.shape[0]
    rim_width = teach_rows // 8
    earlier = shifted(span_ends[-1:], "ctx", 1)
    span_starts = jnp.concatenate([earlier, span_ends[:-1]])
    window = extended(teacher, (("ctx", 0),), rim_width)
    window_start = lax.axis_index("ctx") * teach_rows - rim_width
    positions = window_start + jnp.arange(teach_rows + 2 * rim_width, dtype=jnp.int32)
    member = (positions[None, :] >= span_starts[:, None]) & (
        positions[None, :] < span_ends[:, None]
    )
    sums = jnp.dot(member.astype(jnp.bfloat16), window, preferred_element_type=jnp.float32)
    counts = (span_ends - span_starts).astype(jnp.float32)
    pooled_half = (sums / counts[:, None]).astype(jnp.bfloat16)
    pooled = lax.all_gather(pooled_half, "mp", axis=1, tiled=True)
    projected = jnp.dot(pooled, projector, preferred_element_type=jnp.float32)
    hidden = student_hidden[0].astype(jnp.float32)
    inner, psq, hsq = lax.psum(
        (
            jnp.sum(projected * hidden, axis=1),
            jnp.sum(projected * projected, axis=1),
            jnp.sum(hidden * hidden, axis=1),
        ),
        "mp",
    )
    scale = lax.rsqrt((psq + epsilon) * (hsq + epsilon))
    token_loss = (1.0 - inner * scale)[None, :]
    proj_grad = (
        (inner * scale / (psq + epsilon))[:, None] * projected - scale[:, None] * hidden
    ).astype(jnp.bfloat16)
    w_grad = lax.psum_scatter(
        lax.dot_general(
            pooled, proj_grad, (((0,), (0,)), ((), ())), preferred_element_type=jnp.float32
        ),
        ("ctx", "dp"),
        scatter_dimension=0,
        tiled=True,
    )
    return (token_loss, w_grad)


def solution(mesh):
    sizes = tuple(mesh.shape[axis] for axis in ("ctx", "dp", "mp"))
    return jax.shard_map(
        fused if sizes == (4, 2, 2) else body,
        mesh=mesh,
        in_specs=(
            P("dp", ("groups", "ctx"), "mp"),
            P("dp", ("groups", "ctx"), "mp"),
            P(None, "mp"),
            P("dp", ("groups", "ctx")),
        ),
        out_specs=(P("dp", ("groups", "ctx")), P(("groups", "ctx", "dp"), "mp")),
        check_vma=False,
    )
```
